1024 devices in a mesh: prow: 64 (over x, z), pcol: 16 (over y, core).
Axes of the slice: x: 8, y: 8, z: 8, core: 2. Of those that a mesh axis runs over, the one named last changes fastest.
Arguments:
- rhs_first: float32 [8192, 256], P('prow'), may hold values from -6 to 6
- rhs_second: float32 [8192, 256], P('prow'), may hold values from -6 to 6
- rhs_rest: float32 [90112, 256], P(('prow', 'pcol')), may hold values from -6 to 6
- inverse_first: bfloat16 [8192, 8192], P('pcol', 'prow'), as said below
- inverse_second: bfloat16 [8192, 8192], P('pcol', 'prow'), as said below
- panel_cross: bfloat16 [8192, 8192], P('prow', 'pcol'), may hold values from -0.0625 to 0.0625
- panel_first_rest: bfloat16 [90112, 8192], P('prow', 'pcol'), may hold values from -0.1875 to 0.1875
- panel_second_rest: bfloat16 [90112, 8192], P('prow', 'pcol'), may hold values from -0.1875 to 0.1875
Outputs:
- solved_first: float32 [8192, 256], P('pcol')
- solved_second: float32 [8192, 256], P('pcol')
- remaining: float32 [90112, 256], P(('prow', 'pcol'))
The draws below stay inside these ranges and needn't reach their ends.
Inputs may be any that keep to these rules, and one draw needn't show every extreme that they name: `inverse_first`: lower triangular: entry (i, j) is zero for j > i; the diagonal entries lie between 1 and 2. `inverse_second`: lower triangular: entry (i, j) is zero for j > i; the diagonal entries lie between 1 and 2.
All inputs are finite; a program needn't handle non-finite values.
Results may differ from the reference program's by a relative error of at most 0.005.
Values sent between devices are 32-bit elements; how exact they have to be, the bound alone decides.
A program may use at most 32 MiB of HBM per device.

```python
import jax
import jax.numpy as jnp

NB = 8192
NRHS = 256
TRAIL = 90112


def assemble_lower(key, lower_part):
    row_index = jnp.arange(NB)[:, None]
    col_index = jnp.arange(NB)[None, :]
    diagonal_values = jax.random.uniform(key, (NB,), jnp.float32, 1.0, 2.0)
    diagonal_full = jnp.broadcast_to(diagonal_values[:, None], (NB, NB))
    scaled = lower_part * float(NB) ** (-0.5)
    matrix = jnp.where(row_index > col_index, scaled, jnp.where(row_index == col_index, diagonal_full, 0.0))
    return matrix.astype(jnp.bfloat16)


def draw_inverse_first(key, part):
    key = jax.random.fold_in(key, 11)
    first_key, second_key = jax.random.split(key)
    lower_part = jax.random.truncated_normal(first_key, -4.0, 4.0, (NB, NB), jnp.float32) * 1.5
    return assemble_lower(second_key, lower_part)


def draw_inverse_second(key, part):
    key = jax.random.fold_in(key, 23)
    first_key, second_key = jax.random.split(key)
    lower_part = jax.random.truncated_normal(first_key, -4.0, 4.0, (NB, NB), jnp.float32) * 1.5
    return assemble_lower(second_key, lower_part)


def raised(array, rng, source, target, blocks, factor):
    owner, partner = [(jnp.arange(array.shape[position]) // (array.shape[position] // blocks)).reshape([-1 if axis == position else 1 for axis in range(array.ndim)]) for position in (source, target)]
    chosen = jax.random.permutation(rng, blocks)[partner]
    strong = (owner == chosen) | (owner == (partner + blocks // 2) % blocks)
    return jnp.where(strong, factor * array, array)


def shard_levels(key, extent, pieces, smallest, high):
    gain = 1.0
    for axis_at, parts in pieces:
        steps = jax.random.uniform(jax.random.fold_in(jax.random.fold_in(key, 6), axis_at), (parts,), jnp.float32, smallest / len(pieces), high / len(pieces))
        gain = gain * jnp.repeat(jnp.exp(steps), extent[axis_at] // parts).reshape((-1,) + (1,) * (len(extent) - 1 - axis_at))
    return gain


def gaussian(rng, extent, spread, bound, cuts=(), held_as=jnp.bfloat16):
    entries = jax.random.normal(rng, extent, jnp.float32) * spread
    if len(cuts) > 0:
        entries = shard_levels(rng, extent, cuts, -0.22, 0.18) * entries
    return jnp.clip(entries, min=-bound, max=bound).astype(held_as)


def heavy_noise(key, shape, spread, bound, pieces, heavy, held_as=jnp.bfloat16):
    array = spread * jax.random.normal(key, shape, jnp.float32)
    if pieces:
        array = array * shard_levels(key, shape, pieces, -0.22, 0.18)
    return jnp.clip(raised(array, jax.random.fold_in(key, 3), *heavy), -bound, bound).astype(held_as)


def setup_inputs(seed: int = 0) -> dict:
    streams_of = jax.random.split(jax.random.key(seed), 9)
    rhs_first = gaussian(streams_of[0], (NB, NRHS), 1.0, 6.0, ((0, 64),), jnp.float32)
    rhs_second = gaussian(streams_of[1], (NB, NRHS), 1.0, 6.0, ((0, 64),), jnp.float32)
    rhs_rest = gaussian(streams_of[2], (TRAIL, NRHS), 1.0, 6.0, ((0, 1024),), jnp.float32)
    inverse_first = draw_inverse_first(jax.random.fold_in(streams_of[8], 71), 0)
    inverse_second = draw_inverse_second(jax.random.fold_in(streams_of[8], 71), 0)
    panel_cross = gaussian(streams_of[5], (NB, NB), NB ** -0.5, 0.0625, ((0, 64), (1, 16)))
    panel_first_rest = heavy_noise(streams_of[6], (TRAIL, NB), NB ** -0.5, 0.1875, ((0, 64), (1, 16)), (1, 0, 64, 4.0))
    panel_second_rest = heavy_noise(streams_of[7], (TRAIL, NB), NB ** -0.5, 0.1875, ((0, 64), (1, 16)), (1, 0, 64, 4.0))
    return dict(rhs_first=rhs_first, rhs_second=rhs_second, rhs_rest=rhs_rest, inverse_first=inverse_first, inverse_second=inverse_second, panel_cross=panel_cross, panel_first_rest=panel_first_rest, panel_second_rest=panel_second_rest)


def reference(rhs_first, rhs_second, rhs_rest, inverse_first, inverse_second, panel_cross, panel_first_rest, panel_second_rest):
    solved_first = jnp.dot(inverse_first, rhs_first.astype(jnp.bfloat16), preferred_element_type=jnp.float32)
    first_rounded = solved_first.astype(jnp.bfloat16)
    second_rows = rhs_second - jnp.dot(panel_cross, first_rounded, preferred_element_type=jnp.float32)
    solved_second = jnp.dot(inverse_second, second_rows.astype(jnp.bfloat16), preferred_element_type=jnp.float32)
    second_rounded = solved_second.astype(jnp.bfloat16)
    update_first = jnp.dot(panel_first_rest, first_rounded, preferred_element_type=jnp.float32)
    update_second = jnp.dot(panel_second_rest, second_rounded, preferred_element_type=jnp.float32)
    remaining = rhs_rest - (update_first + update_second)
    return solved_first, solved_second, remaining
```

```python
import jax
import jax.numpy as jnp
from jax import lax
from jax.experimental import pallas as pl
from jax.experimental.pallas import tpu as pltpu
from jax.sharding import PartitionSpec as P

MESH = pl.DeviceIdType.MESH
F32 = jnp.float32
BF16 = jnp.bfloat16
NX = 8
FAR_FIRST = (4, 3, 5, 2, 6, 1, 7)


def kernel(
    r1_hbm, r2_hbm, rest_hbm, inv1_hbm, inv2_hbm, cross_hbm, pf_hbm, ps_hbm,
    o1_hbm, o2_hbm, o3_hbm,
    r1, r2, rest, inv1, inv2, cross, pf, ps,
    part, rs1, mid, rs2, full, rounded,
    cpart, cin, csum, yrs, sec,
    acc, pin, psum, yrs3, out,
    load_sem, store_sem, send_sem, recv_sem, pin_sem,
):
    r = lax.axis_index("prow")
    p = lax.axis_index("pcol")
    x, z = r // NX, r % NX
    y, c = p // 2, p % 2

    def at_x(k):
        return (lax.rem(x + k, NX) * NX + z, p)

    def at_z(k):
        return (x * NX + lax.rem(z + k, NX), p)

    def at_y(k):
        return (r, lax.rem(y + k, NX) * 2 + c)

    partner = (r, y * 2 + (1 - c))
    line = (at_x, at_z)

    loads = []
    for i, (src, dst) in enumerate(
        ((inv1_hbm, inv1), (r1_hbm, r1), (cross_hbm, cross), (r2_hbm, r2),
         (inv2_hbm, inv2), (pf_hbm, pf), (ps_hbm, ps), (rest_hbm, rest))
    ):
        cp = pltpu.make_async_copy(src, dst, load_sem.at[i])
        cp.start()
        loads.append(cp)

    barrier = pltpu.get_barrier_semaphore()
    for k in range(1, NX):
        for to in (at_x, at_z, at_y):
            pl.semaphore_signal(barrier, inc=1, device_id=to(k), device_id_type=MESH)
    pl.semaphore_signal(barrier, inc=1, device_id=partner, device_id_type=MESH)

    sent = []

    def send(src, dst, group, device, recv=None):
        pltpu.make_async_remote_copy(
            src_ref=src,
            dst_ref=dst,
            send_sem=send_sem.at[group],
            recv_sem=recv_sem.at[group] if recv is None else recv,
            device_id=device,
            device_id_type=MESH,
        ).start()

    def wait_bytes(ref, sem):
        pltpu.make_async_copy(ref, ref, sem).wait()

    def arrived(ref, group):
        wait_bytes(ref, recv_sem.at[group])
        sent.append((ref, group))

    loads[0].wait()
    loads[1].wait()

    def solve(b, inverse, values, after_first_sends=None):
        base = 8 * b
        total = jnp.dot(inverse[...], values.astype(BF16), preferred_element_type=F32)
        part[b, 0] = total[:, :128]
        part[b, 1] = total[:, 128:]
        if b == 0:
            pl.semaphore_wait(barrier, 3 * (NX - 1) + 1)
        mine = (x, z)
        for k in FAR_FIRST:
            for h in range(2):
                to = lax.rem(mine[h] + k, NX)
                send(part.at[b, h, pl.ds(pl.multiple_of(to * 64, 64), 64)], rs1.at[b, h, k - 1], base + h, line[h](k))
        if after_first_sends is not None:
            after_first_sends()
        for h in range(2):
            arrived(rs1.at[b, h], base + h)
            s = part[b, h, pl.ds(pl.multiple_of(mine[h] * 64, 64), 64)]
            for k in range(1, NX):
                s = s + rs1[b, h, k - 1]
            mid[b, h] = s
            other = mine[1 - h]
            for k in FAR_FIRST:
                to = lax.rem(other + k, NX)
                send(mid.at[b, h, pl.ds(pl.multiple_of(to * 8, 8), 8)], rs2.at[b, h, k - 1], base + 2 + h, line[1 - h](k))
        for h in range(2):
            other = mine[1 - h]
            arrived(rs2.at[b, h], base + 2 + h)
            s = mid[b, h, pl.ds(pl.multiple_of(other * 8, 8), 8)]
            for k in range(1, NX):
                s = s + rs2[b, h, k - 1]
            row = pl.multiple_of(mine[h] * 64 + other * 8, 8)
            full[b, h, pl.ds(row, 8)] = s
            for k in FAR_FIRST:
                here = full.at[b, h, pl.ds(row, 8)]
                send(here, here, base + 4 + h, line[1 - h](k))
        for h in range(2):
            arrived(full.at[b, h, pl.ds(0, 56)], base + 4 + h)
            for k in FAR_FIRST:
                here = full.at[b, h, pl.ds(pl.multiple_of(mine[h] * 64, 64), 64)]
                send(here, here, base + 6 + h, line[h](k))
        for h in range(2):
            arrived(full.at[b, h, pl.ds(0, 448)], base + 6 + h)
            rounded[b, :, h * 128 : (h + 1) * 128] = full[b, h].astype(BF16)

    def store(b, out_hbm):
        cps = []
        for h in range(2):
            cp = pltpu.make_async_copy(full.at[b, h], out_hbm.at[:, pl.ds(h * 128, 128)], store_sem.at[2 * b + h])
            cp.start()
            cps.append(cp)
        return cps

    solve(0, inv1, r1[...])

    g = 16
    loads[2].wait()
    cpart[...] = jnp.dot(cross[...], rounded[0], preferred_element_type=F32)
    send(cpart.at[pl.ds(pl.multiple_of((1 - c) * 64, 64), 64)], cin, g, partner)
    arrived(cin, g)
    csum[...] = cpart[pl.ds(pl.multiple_of(c * 64, 64), 64)] + cin[...]
    for k in FAR_FIRST:
        to = lax.rem(y + k, NX)
        send(csum.at[pl.ds(pl.multiple_of(to * 8, 8), 8)], yrs.at[k - 1], g + 1, at_y(k))
    stores = store(0, o1_hbm)
    loads[3].wait()
    loads[4].wait()
    loads[5].wait()

    def first_update(i, carry):
        acc[i] = jnp.dot(
            pf[pl.ds(pl.multiple_of(i * 176, 176), 176)], rounded[0], preferred_element_type=F32
        ).reshape(2, 88, 256)
        return carry

    lax.fori_loop(0, NX, first_update, 0)
    arrived(yrs, g + 1)
    s = csum[pl.ds(pl.multiple_of(y * 8, 8), 8)]
    for k in range(1, NX):
        s = s + yrs[k - 1]
    row = pl.multiple_of(c * 64 + y * 8, 8)
    sec[pl.ds(row, 8)] = r2[pl.ds(row, 8)] - s
    for k in FAR_FIRST:
        here = sec.at[pl.ds(row, 8)]
        send(here, here, g + 2, at_y(k))
    arrived(sec.at[pl.ds(0, 56)], g + 2)
    here = sec.at[pl.ds(pl.multiple_of(c * 64, 64), 64)]
    send(here, here, g + 3, partner)
    arrived(sec.at[pl.ds(0, 64)], g + 3)

    solve(1, inv2, sec[...])

    loads[6].wait()
    for k in FAR_FIRST + (0,):
        to = lax.rem(y + k, NX)
        acc[to] = acc[to] + jnp.dot(
            ps[pl.ds(pl.multiple_of(to * 176, 176), 176)], rounded[1], preferred_element_type=F32
        ).reshape(2, 88, 256)
        send(acc.at[to, 1 - c], pin.at[k], g + 4, partner, pin_sem.at[k])
    stores += store(1, o2_hbm)
    for k in FAR_FIRST:
        to = lax.rem(y + k, NX)
        wait_bytes(pin.at[k], pin_sem.at[k])
        psum[k] = acc[to, c] + pin[k]
        send(psum.at[k], yrs3.at[k - 1], g + 5, at_y(k))
    wait_bytes(pin.at[0], pin_sem.at[0])
    loads[7].wait()
    s = acc[y, c] + pin[0]
    arrived(yrs3, g + 5)
    for k in range(1, NX):
        s = s + yrs3[k - 1]
    out[...] = rest[...] - s
    cp = pltpu.make_async_copy(out, o3_hbm, store_sem.at[4])
    cp.start()
    stores.append(cp)
    for ref, group in sent:
        wait_bytes(ref, send_sem.at[group])
    wait_bytes(pin, send_sem.at[g + 4])
    for cp in stores:
        cp.wait()


def solution(mesh):
    def local(rhs_first, rhs_second, rhs_rest, inverse_first, inverse_second, panel_cross, panel_first, panel_second):
        any_spec = pl.BlockSpec(memory_space=pltpu.HBM)
        arguments = (rhs_first, rhs_second, rhs_rest, inverse_first, inverse_second, panel_cross, panel_first, panel_second)
        return pl.pallas_call(
            kernel,
            out_shape=(
                jax.ShapeDtypeStruct((512, 256), F32),
                jax.ShapeDtypeStruct((512, 256), F32),
                jax.ShapeDtypeStruct((88, 256), F32),
            ),
            in_specs=[any_spec] * 8,
            out_specs=(any_spec,) * 3,
            scratch_shapes=[pltpu.VMEM(a.shape, a.dtype) for a in arguments]
            + [
                pltpu.VMEM((2, 2, 512, 128), F32),
                pltpu.VMEM((2, 2, 7, 64, 128), F32),
                pltpu.VMEM((2, 2, 64, 128), F32),
                pltpu.VMEM((2, 2, 7, 8, 128), F32),
                pltpu.VMEM((2, 2, 512, 128), F32),
                pltpu.VMEM((2, 512, 256), BF16),
                pltpu.VMEM((128, 256), F32),
                pltpu.VMEM((64, 256), F32),
                pltpu.VMEM((64, 256), F32),
                pltpu.VMEM((7, 8, 256), F32),
                pltpu.VMEM((128, 256), F32),
                pltpu.VMEM((8, 2, 88, 256), F32),
                pltpu.VMEM((8, 88, 256), F32),
                pltpu.VMEM((8, 88, 256), F32),
                pltpu.VMEM((7, 88, 256), F32),
                pltpu.VMEM((88, 256), F32),
                pltpu.SemaphoreType.DMA((8,)),
                pltpu.SemaphoreType.DMA((5,)),
                pltpu.SemaphoreType.DMA((24,)),
                pltpu.SemaphoreType.DMA((24,)),
                pltpu.SemaphoreType.DMA((8,)),
            ],
            compiler_params=pltpu.CompilerParams(
                collective_id=0, has_side_effects=True, vmem_limit_bytes=60 * 2**20
            ),
            cost_estimate=pl.CostEstimate(flops=10**9, bytes_accessed=5 * 10**6, transcendentals=0),
        )(*arguments)

    in_specs = (
        P("prow", None),
        P("prow", None),
        P(("prow", "pcol"), None),
        P("pcol", "prow"),
        P("pcol", "prow"),
        P("prow", "pcol"),
        P("prow", "pcol"),
        P("prow", "pcol"),
    )
    out_specs = (P("pcol", None), P("pcol", None), P(("prow", "pcol"), None))
    return jax.shard_map(local, mesh=mesh, in_specs=in_specs, out_specs=out_specs, check_vma=False)
```

```python
import jax
import jax.numpy as jnp
from jax import lax
from jax.experimental import pallas as pl
from jax.experimental.pallas import tpu as pltpu
from jax.sharding import PartitionSpec as P

MESH = pl.DeviceIdType.MESH
F32 = jnp.float32
BF16 = jnp.bfloat16
NX = 8
FAR_FIRST = (4, 3, 5, 2, 6, 1, 7)
N_GROUPS = 44
PIECES = (pl.ds(0, 48), pl.ds(48, 40))


def kernel(
    r1_hbm, r2_hbm, rest_hbm, inv1_hbm, inv2_hbm, cross_hbm, pf_hbm, ps_hbm,
    o1_hbm, o2_hbm, o3_hbm,
    r1, r2, rest, inv1, inv2, cross, pf, ps,
    part, rs1, mid, rs2, full, rounded,
    cpart, yrs, sec,
    acc, pin, ring_in, ring_out, out,
    load_sem, store_sem, send_sem, recv_sem, pin_sem, ring_sem,
):
    r = lax.axis_index("prow")
    p = lax.axis_index("pcol")
    x, z = r // NX, r % NX
    y, c = p // 2, p % 2
    mine = (x, z)

    def at_x(k):
        return (lax.rem(x + k, NX) * NX + z, p)

    def at_z(k):
        return (x * NX + lax.rem(z + k, NX), p)

    def at_y(k, other_core=0):
        return (r, lax.rem(y + k, NX) * 2 + (1 - c if other_core else c))

    partner = at_y(0, 1)
    column = [(k, f) for k in FAR_FIRST for f in range(2)] + [(0, 1)]
    line = (at_x, at_z)

    def rows(start, count):
        return pl.ds(pl.multiple_of(start, 8), count)

    loads = []
    for i, (src, dst) in enumerate(
        ((inv1_hbm, inv1), (r1_hbm, r1), (cross_hbm, cross), (r2_hbm, r2),
         (inv2_hbm, inv2), (pf_hbm, pf), (ps_hbm, ps), (rest_hbm, rest))
    ):
        cp = pltpu.make_async_copy(src, dst, load_sem.at[i])
        cp.start()
        loads.append(cp)

    barrier = pltpu.get_barrier_semaphore()
    for k in range(1, NX):
        for to in line:
            pl.semaphore_signal(barrier, inc=1, device_id=to(k), device_id_type=MESH)
    for k, f in column:
        pl.semaphore_signal(barrier, inc=1, device_id=at_y(k, f), device_id_type=MESH)

    def send(src, dst, group, device, recv=None):
        pltpu.make_async_remote_copy(
            src_ref=src,
            dst_ref=dst,
            send_sem=send_sem.at[group],
            recv_sem=recv_sem.at[group] if recv is None else recv,
            device_id=device,
            device_id_type=MESH,
        ).start()

    def wait_bytes(ref, sem):
        pltpu.make_async_copy(ref, ref, sem).wait()

    at_end = []
    stores = []

    def arrived(ref, group):
        wait_bytes(ref, recv_sem.at[group])
        at_end.append(lambda: wait_bytes(ref, send_sem.at[group]))

    def on_owner(h, s, yes, no):
        owner = lax.rem(mine[1 - h], 2) == s
        pl.when(owner)(yes)
        if no is not None:
            pl.when(jnp.logical_not(owner))(no)

    def solve(b, s):
        def group(stage, h):
            return ((b * 2 + s) * 4 + stage) * 2 + h

        if s == 1:
            for h in range(2):
                wait_bytes(rs1.at[b, 0, h], send_sem.at[(b * 16 + 0) + h])
        for k in FAR_FIRST:
            for h in range(2):
                to = lax.rem(mine[h] + k, NX)
                send(part.at[b, s, rows(h * 256 + to * 32, 32)], rs1.at[b, s, h, k - 1], group(0, h), line[h](k))
        yield
        for h in range(2):
            if s == 1:
                arrived(rs1.at[b, s, h], group(0, h))
            else:
                wait_bytes(rs1.at[b, s, h], recv_sem.at[group(0, h)])
            value = part[b, s, rows(h * 256 + mine[h] * 32, 32)]
            for k in range(1, NX):
                value = value + rs1[b, s, h, k - 1]
            mid[b, s, h] = value
            other = mine[1 - h]

            def spread(ks, h=h, other=other):
                for k in ks:
                    to = lax.rem(other + k, NX)
                    send(mid.at[b, s, h, rows(to // 2 * 8, 8)], rs2.at[b, s, h, k - 1], group(1, h), line[1 - h](k))

            on_owner(h, s, lambda: spread((4, 2, 6)), lambda: spread((3, 5, 1, 7)))
        yield
        for h in range(2):
            other = mine[1 - h]

            def finish(h=h, other=other):
                wait_bytes(rs2.at[b, s, h], recv_sem.at[group(1, h)])
                value = mid[b, s, h, rows(other // 2 * 8, 8)]
                for k in range(1, NX):
                    value = value + rs2[b, s, h, k - 1]
                place = rows(h * 256 + mine[h] * 32 + other // 2 * 8, 8)
                full[b, s, place] = value
                here = full.at[b, s, place]
                for k in FAR_FIRST:
                    send(here, here, group(2, h), line[1 - h](k))

            on_owner(h, s, finish, None)
        yield
        for h in range(2):

            def gathered(count, h=h):
                wait_bytes(full.at[b, s, pl.ds(0, count)], recv_sem.at[group(2, h)])

            on_owner(h, s, lambda: gathered(24), lambda: gathered(32))
            here = full.at[b, s, rows(h * 256 + mine[h] * 32, 32)]
            for k in FAR_FIRST:
                send(here, here, group(3, h), line[h](k))

            def leave(owner, h=h):
                wait_bytes(mid.at[b, s, h, pl.ds(0, 24 if owner else 32)], send_sem.at[group(1, h)])
                if owner:
                    wait_bytes(full.at[b, s, pl.ds(0, 56)], send_sem.at[group(2, h)])

            at_end.append(lambda h=h, leave=leave: on_owner(h, s, lambda: leave(True), lambda: leave(False)))
        yield
        for h in range(2):
            arrived(full.at[b, s, pl.ds(0, 224)], group(3, h))
        rounded[b, :, s * 128 : (s + 1) * 128] = full[b, s].astype(BF16)

    def store(b, s, out_hbm):
        cp = pltpu.make_async_copy(full.at[b, s], out_hbm.at[:, pl.ds(s * 128, 128)], store_sem.at[2 * b + s])
        cp.start()
        stores.append(cp)

    def first_update(i, carry):
        update = jnp.dot(pf[pl.ds(pl.multiple_of(i * 176, 176), 176)], rounded[0], preferred_element_type=F32)
        for core in range(2):
            for h in range(2):
                acc[i, core, h] = update[core * 88 : (core + 1) * 88, h * 128 : (h + 1) * 128]
        return carry

    up, down = at_y(1), at_y(NX - 1)

    def stream(s):
        columns = slice(s * 128, (s + 1) * 128)
        yield from solve(0, s)

        g = 32 + 4 * s
        if s == 0:
            loads[2].wait()
        cpart[s] = jnp.dot(cross[...], rounded[0, :, columns], preferred_element_type=F32)
        for k, f in column:
            to = at_y(k, f)
            send(cpart.at[s, rows(to[1] * 8, 8)], yrs.at[s, 2 * k + f - 1], g, to)
        store(0, s, o1_hbm)
        if s == 1:
            loads[5].wait()
            lax.fori_loop(0, 2, first_update, 0)
        yield
        if s == 0:
            loads[3].wait()
        arrived(yrs.at[s], g)
        place = rows(p * 8, 8)
        value = cpart[s, place]
        for i in range(15):
            value = value + yrs[s, i]
        sec[s, place] = r2[place, columns] - value
        here = sec.at[s, place]
        for k, f in column:
            send(here, here, g + 1, at_y(k, f))
        if s == 1:
            lax.fori_loop(2, 4, first_update, 0)
        yield
        if s == 0:
            loads[4].wait()
        arrived(sec.at[s, pl.ds(0, 120)], g + 1)
        part[1, s] = jnp.dot(inv2[...], sec[s].astype(BF16), preferred_element_type=F32)
        solving = solve(1, s)
        next(solving)
        if s == 1:
            lax.fori_loop(4, 8, first_update, 0)
        yield
        yield from solving

        store(1, s, o2_hbm)
        if s == 0:
            loads[6].wait()

        def second_update(ks):
            for k in ks:
                to = lax.rem(y + k, NX)
                update = jnp.dot(ps[pl.ds(pl.multiple_of(to * 176, 176), 176)], rounded[1, :, columns], preferred_element_type=F32)
                for core in range(2):
                    acc[to, core, s] += update[core * 88 : (core + 1) * 88]
                send(acc.at[to, 1 - c, s], pin.at[k, s], 40 + s, partner, pin_sem.at[k, s])

        ready = set()

        def summed(k, part_rows):
            if k not in ready:
                wait_bytes(pin.at[k, s], pin_sem.at[k, s])
                ready.add(k)
            return acc[lax.rem(y + k, NX), c, s, part_rows] + pin[k, s, part_rows]

        slots = iter(range(7))

        def pass_on(step, way):
            slot = next(slots)
            for i, part_rows in enumerate(PIECES):
                value = summed(5 - step if way == 0 else NX - (5 - step), part_rows)
                if step > (1 if way == s else 2):
                    come = ring_in.at[way, step - 2, s, part_rows]
                    wait_bytes(come, ring_sem.at[way, step - 2, s, i])
                    value = value + come[...]
                ring_out[s, slot, part_rows] = value
                send(
                    ring_out.at[s, slot, part_rows], ring_in.at[way, step - 1, s, part_rows], 42 + s,
                    (up, down)[way], ring_sem.at[way, step - 1, s, i],
                )

        second_update((4, 3, 5, 2) if s == 0 else (4, 5, 3, 6))
        pass_on(1, s)
        pass_on(2, 1 - s)
        second_update((6, 1, 7, 0) if s == 0 else (2, 7, 1, 0))
        yield
        pass_on(2, s)
        yield
        pass_on(3, 1 - s)
        pass_on(3, s)
        yield
        pass_on(4, 1 - s)
        pass_on(4, s)
        yield
        if s == 0:
            loads[7].wait()
        for i, part_rows in enumerate(PIECES):
            value = summed(0, part_rows)
            for way in range(2):
                come = ring_in.at[way, 3, s, part_rows]
                wait_bytes(come, ring_sem.at[way, 3, s, i])
                value = value + come[...]
            out[s, part_rows] = rest[part_rows, columns] - value
        cp = pltpu.make_async_copy(out.at[s], o3_hbm.at[:, pl.ds(s * 128, 128)], store_sem.at[4 + s])
        cp.start()
        stores.append(cp)
        at_end.append(lambda: wait_bytes(pin.at[:, s], send_sem.at[40 + s]))
        at_end.append(lambda: wait_bytes(ring_out.at[s], send_sem.at[42 + s]))

    loads[0].wait()
    loads[1].wait()
    total = jnp.dot(inv1[...], r1[...].astype(BF16), preferred_element_type=F32)
    part[0, 0] = total[:, :128]
    part[0, 1] = total[:, 128:]
    pl.semaphore_wait(barrier, 2 * (NX - 1) + len(column))
    streams = [stream(0), stream(1)]
    while streams:
        for one in list(streams):
            try:
                next(one)
            except StopIteration:
                streams.remove(one)
    for end in at_end:
        end()
    for cp in stores:
        cp.wait()


def copy_kernel(a1, a2, a3, b1, b2, b3, v1, v2, v3, in_sem, out_sem):
    pieces = [(a3, v3, b3)]
    for i in range(4):
        rows = pl.ds(i * 128, 128)
        pieces += [(a1.at[rows], v1.at[rows], b1.at[rows]), (a2.at[rows], v2.at[rows], b2.at[rows])]
    come = [pltpu.make_async_copy(a, v, in_sem.at[i]) for i, (a, v, b) in enumerate(pieces)]
    go = [pltpu.make_async_copy(v, b, out_sem.at[i]) for i, (a, v, b) in enumerate(pieces)]
    for cp in come:
        cp.start()
    for cp, then in zip(come, go):
        cp.wait()
        then.start()
    for cp in go:
        cp.wait()


def solution(mesh):
    def local(rhs_first, rhs_second, rhs_rest, inverse_first, inverse_second, panel_cross, panel_first, panel_second):
        any_spec = pl.BlockSpec(memory_space=pltpu.HBM)
        arguments = (rhs_first, rhs_second, rhs_rest, inverse_first, inverse_second, panel_cross, panel_first, panel_second)
        shapes = (
            jax.ShapeDtypeStruct((512, 256), F32),
            jax.ShapeDtypeStruct((512, 256), F32),
            jax.ShapeDtypeStruct((88, 256), F32),
        )
        results = pl.pallas_call(
            kernel,
            out_shape=shapes,
            in_specs=[any_spec] * 8,
            out_specs=(any_spec,) * 3,
            scratch_shapes=[pltpu.VMEM(a.shape, a.dtype) for a in arguments]
            + [
                pltpu.VMEM((2, 2, 512, 128), F32),
                pltpu.VMEM((2, 2, 2, 7, 32, 128), F32),
                pltpu.VMEM((2, 2, 2, 32, 128), F32),
                pltpu.VMEM((2, 2, 2, 7, 8, 128), F32),
                pltpu.VMEM((2, 2, 512, 128), F32),
                pltpu.VMEM((2, 512, 256), BF16),
                pltpu.VMEM((2, 128, 128), F32),
                pltpu.VMEM((2, 15, 8, 128), F32),
                pltpu.VMEM((2, 128, 128), F32),
                pltpu.VMEM((8, 2, 2, 88, 128), F32),
                pltpu.VMEM((8, 2, 88, 128), F32),
                pltpu.VMEM((2, 4, 2, 88, 128), F32),
                pltpu.VMEM((2, 7, 88, 128), F32),
                pltpu.VMEM((2, 88, 128), F32),
                pltpu.SemaphoreType.DMA((8,)),
                pltpu.SemaphoreType.DMA((6,)),
                pltpu.SemaphoreType.DMA((N_GROUPS,)),
                pltpu.SemaphoreType.DMA((N_GROUPS,)),
                pltpu.SemaphoreType.DMA((8, 2)),
                pltpu.SemaphoreType.DMA((2, 4, 2, len(PIECES))),
            ],
            compiler_params=pltpu.CompilerParams(
                collective_id=0, has_side_effects=True, vmem_limit_bytes=60 * 2**20
            ),
            cost_estimate=pl.CostEstimate(flops=10**9, bytes_accessed=5 * 10**6, transcendentals=0),
        )(*arguments)
        return pl.pallas_call(
            copy_kernel,
            out_shape=shapes,
            in_specs=[any_spec] * 3,
            out_specs=(any_spec,) * 3,
            scratch_shapes=[pltpu.VMEM(a.shape, a.dtype) for a in shapes]
            + [pltpu.SemaphoreType.DMA((9,)), pltpu.SemaphoreType.DMA((9,))],
            compiler_params=pltpu.CompilerParams(vmem_limit_bytes=60 * 2**20),
        )(*results)

    in_specs = (
        P("prow", None),
        P("prow", None),
        P(("prow", "pcol"), None),
        P("pcol", "prow"),
        P("pcol", "prow"),
        P("prow", "pcol"),
        P("prow", "pcol"),
        P("prow", "pcol"),
    )
    out_specs = (P("pcol", None), P("pcol", None), P(("prow", "pcol"), None))
    return jax.shard_map(local, mesh=mesh, in_specs=in_specs, out_specs=out_specs, check_vma=False)
```

```python
import jax
import jax.numpy as jnp
from jax import lax
from jax.experimental import pallas as pl
from jax.experimental.pallas import tpu as pltpu
from jax.sharding import PartitionSpec as P

MESH = pl.DeviceIdType.MESH
F32 = jnp.float32
BF16 = jnp.bfloat16
NX = 8
FAR_FIRST = (4, 3, 5, 2, 6, 1, 7)
N_GROUPS = 44
PIECES = (pl.ds(0, 48), pl.ds(48, 40))


def kernel(
    r1_hbm, r2_hbm, rest_hbm, inv1_hbm, inv2_hbm, cross_hbm, pf_hbm, ps_hbm,
    o1_hbm, o2_hbm, o3_hbm,
    r1, r2, rest, inv1, inv2, cross, pf, ps,
    part, rs1, mid, rs2, full, rounded,
    cpart, yrs, sec,
    acc, pin, ring_in, ring_out, out,
    load_sem, store_sem, send_sem, recv_sem, pin_sem, ring_sem,
):
    r = lax.axis_index("prow")
    p = lax.axis_index("pcol")
    x, z = r // NX, r % NX
    y, c = p // 2, p % 2
    mine = (x, z)

    def at_x(k):
        return (lax.rem(x + k, NX) * NX + z, p)

    def at_z(k):
        return (x * NX + lax.rem(z + k, NX), p)

    def at_y(k, other_core=0):
        return (r, lax.rem(y + k, NX) * 2 + (1 - c if other_core else c))

    partner = at_y(0, 1)
    column = [(k, f) for k in FAR_FIRST for f in range(2)] + [(0, 1)]
    line = (at_x, at_z)

    def rows(start, count):
        return pl.ds(pl.multiple_of(start, 8), count)

    loads = []
    for i, (src, dst) in enumerate(
        ((inv1_hbm, inv1), (r1_hbm, r1), (cross_hbm, cross), (r2_hbm, r2),
         (inv2_hbm, inv2), (pf_hbm, pf), (ps_hbm, ps), (rest_hbm, rest))
    ):
        cp = pltpu.make_async_copy(src, dst, load_sem.at[i])
        cp.start()
        loads.append(cp)

    barrier = pltpu.get_barrier_semaphore()
    for k in range(1, NX):
        for to in line:
            pl.semaphore_signal(barrier, inc=1, device_id=to(k), device_id_type=MESH)
    for k, f in column:
        pl.semaphore_signal(barrier, inc=1, device_id=at_y(k, f), device_id_type=MESH)

    def send(src, dst, group, device, recv=None):
        pltpu.make_async_remote_copy(
            src_ref=src,
            dst_ref=dst,
            send_sem=send_sem.at[group],
            recv_sem=recv_sem.at[group] if recv is None else recv,
            device_id=device,
            device_id_type=MESH,
        ).start()

    def wait_bytes(ref, sem):
        pltpu.make_async_copy(ref, ref, sem).wait()

    at_end = []
    stores = []

    def arrived(ref, group):
        wait_bytes(ref, recv_sem.at[group])
        at_end.append(lambda: wait_bytes(ref, send_sem.at[group]))

    def solve(b, s):
        def group(stage, h):
            return ((b * 2 + s) * 4 + stage) * 2 + h

        if s == 1:
            for h in range(2):
                wait_bytes(rs1.at[b, 0, h], send_sem.at[(b * 16 + 0) + h])
        for k in FAR_FIRST:
            for h in range(2):
                to = lax.rem(mine[h] + k, NX)
                send(part.at[b, s, rows(h * 256 + to * 32, 32)], rs1.at[b, s, h, k - 1], group(0, h), line[h](k))
        yield
        for h in range(2):
            if s == 1:
                arrived(rs1.at[b, s, h], group(0, h))
            else:
                wait_bytes(rs1.at[b, s, h], recv_sem.at[group(0, h)])
            value = part[b, s, rows(h * 256 + mine[h] * 32, 32)]
            for k in range(1, NX):
                value = value + rs1[b, s, h, k - 1]
            other = mine[1 - h]
            mid[b, s, h] = value
            rs2[b, s, h, other] = value
            for k in FAR_FIRST:
                send(mid.at[b, s, h], rs2.at[b, s, h, other], group(1, h), line[1 - h](k))
        yield
        for h in range(2):
            arrived(rs2.at[b, s, h, pl.ds(0, 7)], group(1, h))
            value = rs2[b, s, h, 0]
            for i in range(1, NX):
                value = value + rs2[b, s, h, i]
            place = rows(h * 256 + mine[h] * 32, 32)
            full[b, s, place] = value
            here = full.at[b, s, place]
            for k in FAR_FIRST:
                send(here, here, group(3, h), line[h](k))
        yield
        for h in range(2):
            arrived(full.at[b, s, pl.ds(0, 224)], group(3, h))
        rounded[b, :, s * 128 : (s + 1) * 128] = full[b, s].astype(BF16)

    def store(b, s, out_hbm):
        cp = pltpu.make_async_copy(full.at[b, s], out_hbm.at[:, pl.ds(s * 128, 128)], store_sem.at[2 * b + s])
        cp.start()
        stores.append(cp)

    def first_update(i, carry):
        update = jnp.dot(pf[pl.ds(pl.multiple_of(i * 176, 176), 176)], rounded[0], preferred_element_type=F32)
        for core in range(2):
            for h in range(2):
                acc[i, core, h] = update[core * 88 : (core + 1) * 88, h * 128 : (h + 1) * 128]
        return carry

    up, down = at_y(1), at_y(NX - 1)

    def stream(s):
        columns = slice(s * 128, (s + 1) * 128)
        yield from solve(0, s)

        g = 32 + 4 * s
        if s == 0:
            loads[2].wait()
        cpart[s] = jnp.dot(cross[...], rounded[0, :, columns], preferred_element_type=F32)
        for k, f in column:
            to = at_y(k, f)
            send(cpart.at[s, rows(to[1] * 8, 8)], yrs.at[s, 2 * k + f - 1], g, to)
        store(0, s, o1_hbm)
        if s == 1:
            loads[5].wait()
            lax.fori_loop(0, 2, first_update, 0)
        yield
        if s == 0:
            loads[3].wait()
        arrived(yrs.at[s], g)
        place = rows(p * 8, 8)
        value = cpart[s, place]
        for i in range(15):
            value = value + yrs[s, i]
        sec[s, place] = r2[place, columns] - value
        here = sec.at[s, place]
        for k, f in column:
            send(here, here, g + 1, at_y(k, f))
        if s == 1:
            lax.fori_loop(2, 4, first_update, 0)
        yield
        if s == 0:
            loads[4].wait()
        arrived(sec.at[s, pl.ds(0, 120)], g + 1)
        part[1, s] = jnp.dot(inv2[...], sec[s].astype(BF16), preferred_element_type=F32)
        solving = solve(1, s)
        next(solving)
        if s == 1:
            lax.fori_loop(4, 8, first_update, 0)
        yield
        yield from solving

        store(1, s, o2_hbm)
        if s == 0:
            loads[6].wait()

        def second_update(ks):
            for k in ks:
                to = lax.rem(y + k, NX)
                update = jnp.dot(ps[pl.ds(pl.multiple_of(to * 176, 176), 176)], rounded[1, :, columns], preferred_element_type=F32)
                for core in range(2):
                    acc[to, core, s] += update[core * 88 : (core + 1) * 88]
                send(acc.at[to, 1 - c, s], pin.at[k, s], 40 + s, partner, pin_sem.at[k, s])

        ready = set()

        def summed(k, part_rows):
            if k not in ready:
                wait_bytes(pin.at[k, s], pin_sem.at[k, s])
                ready.add(k)
            return acc[lax.rem(y + k, NX), c, s, part_rows] + pin[k, s, part_rows]

        slots = iter(range(7))

        def pass_on(step, way):
            slot = next(slots)
            for i, part_rows in enumerate(PIECES):
                value = summed(5 - step if way == 0 else NX - (5 - step), part_rows)
                if step > (1 if way == s else 2):
                    come = ring_in.at[way, step - 2, s, part_rows]
                    wait_bytes(come, ring_sem.at[way, step - 2, s, i])
                    value = value + come[...]
                ring_out[s, slot, part_rows] = value
                send(
                    ring_out.at[s, slot, part_rows], ring_in.at[way, step - 1, s, part_rows], 42 + s,
                    (up, down)[way], ring_sem.at[way, step - 1, s, i],
                )

        second_update((4, 3, 5, 2) if s == 0 else (4, 5, 3, 6))
        pass_on(1, s)
        pass_on(2, 1 - s)
        second_update((6, 1, 7, 0) if s == 0 else (2, 7, 1, 0))
        yield
        pass_on(2, s)
        yield
        pass_on(3, 1 - s)
        pass_on(3, s)
        yield
        pass_on(4, 1 - s)
        pass_on(4, s)
        yield
        if s == 0:
            loads[7].wait()
        for i, part_rows in enumerate(PIECES):
            value = summed(0, part_rows)
            for way in range(2):
                come = ring_in.at[way, 3, s, part_rows]
                wait_bytes(come, ring_sem.at[way, 3, s, i])
                value = value + come[...]
            out[s, part_rows] = rest[part_rows, columns] - value
        cp = pltpu.make_async_copy(out.at[s], o3_hbm.at[:, pl.ds(s * 128, 128)], store_sem.at[4 + s])
        cp.start()
        stores.append(cp)
        at_end.append(lambda: wait_bytes(pin.at[:, s], send_sem.at[40 + s]))
        at_end.append(lambda: wait_bytes(ring_out.at[s], send_sem.at[42 + s]))

    loads[0].wait()
    loads[1].wait()
    total = jnp.dot(inv1[...], r1[...].astype(BF16), preferred_element_type=F32)
    part[0, 0] = total[:, :128]
    part[0, 1] = total[:, 128:]
    pl.semaphore_wait(barrier, 2 * (NX - 1) + len(column))
    streams = [stream(0), stream(1)]
    while streams:
        for one in list(streams):
            try:
                next(one)
            except StopIteration:
                streams.remove(one)
    for end in at_end:
        end()
    for cp in stores:
        cp.wait()


def copy_kernel(a1, a2, a3, b1, b2, b3, v1, v2, v3, in_sem, out_sem):
    pieces = [(a3, v3, b3)]
    for i in range(4):
        rows = pl.ds(i * 128, 128)
        pieces += [(a1.at[rows], v1.at[rows], b1.at[rows]), (a2.at[rows], v2.at[rows], b2.at[rows])]
    come = [pltpu.make_async_copy(a, v, in_sem.at[i]) for i, (a, v, b) in enumerate(pieces)]
    go = [pltpu.make_async_copy(v, b, out_sem.at[i]) for i, (a, v, b) in enumerate(pieces)]
    for cp in come:
        cp.start()
    for cp, then in zip(come, go):
        cp.wait()
        then.start()
    for cp in go:
        cp.wait()


def solution(mesh):
    def local(rhs_first, rhs_second, rhs_rest, inverse_first, inverse_second, panel_cross, panel_first, panel_second):
        any_spec = pl.BlockSpec(memory_space=pltpu.HBM)
        arguments = (rhs_first, rhs_second, rhs_rest, inverse_first, inverse_second, panel_cross, panel_first, panel_second)
        shapes = (
            jax.ShapeDtypeStruct((512, 256), F32),
            jax.ShapeDtypeStruct((512, 256), F32),
            jax.ShapeDtypeStruct((88, 256), F32),
        )
        results = pl.pallas_call(
            kernel,
            out_shape=shapes,
            in_specs=[any_spec] * 8,
            out_specs=(any_spec,) * 3,
            scratch_shapes=[pltpu.VMEM(a.shape, a.dtype) for a in arguments]
            + [
                pltpu.VMEM((2, 2, 512, 128), F32),
                pltpu.VMEM((2, 2, 2, 7, 32, 128), F32),
                pltpu.VMEM((2, 2, 2, 32, 128), F32),
                pltpu.VMEM((2, 2, 2, 8, 32, 128), F32),
                pltpu.VMEM((2, 2, 512, 128), F32),
                pltpu.VMEM((2, 512, 256), BF16),
                pltpu.VMEM((2, 128, 128), F32),
                pltpu.VMEM((2, 15, 8, 128), F32),
                pltpu.VMEM((2, 128, 128), F32),
                pltpu.VMEM((8, 2, 2, 88, 128), F32),
                pltpu.VMEM((8, 2, 88, 128), F32),
                pltpu.VMEM((2, 4, 2, 88, 128), F32),
                pltpu.VMEM((2, 7, 88, 128), F32),
                pltpu.VMEM((2, 88, 128), F32),
                pltpu.SemaphoreType.DMA((8,)),
                pltpu.SemaphoreType.DMA((6,)),
                pltpu.SemaphoreType.DMA((N_GROUPS,)),
                pltpu.SemaphoreType.DMA((N_GROUPS,)),
                pltpu.SemaphoreType.DMA((8, 2)),
                pltpu.SemaphoreType.DMA((2, 4, 2, len(PIECES))),
            ],
            compiler_params=pltpu.CompilerParams(
                collective_id=0, has_side_effects=True, vmem_limit_bytes=60 * 2**20
            ),
            cost_estimate=pl.CostEstimate(flops=10**9, bytes_accessed=5 * 10**6, transcendentals=0),
        )(*arguments)
        return pl.pallas_call(
            copy_kernel,
            out_shape=shapes,
            in_specs=[any_spec] * 3,
            out_specs=(any_spec,) * 3,
            scratch_shapes=[pltpu.VMEM(a.shape, a.dtype) for a in shapes]
            + [pltpu.SemaphoreType.DMA((9,)), pltpu.SemaphoreType.DMA((9,))],
            compiler_params=pltpu.CompilerParams(vmem_limit_bytes=60 * 2**20),
        )(*results)

    in_specs = (
        P("prow", None),
        P("prow", None),
        P(("prow", "pcol"), None),
        P("pcol", "prow"),
        P("pcol", "prow"),
        P("prow", "pcol"),
        P("prow", "pcol"),
        P("prow", "pcol"),
    )
    out_specs = (P("pcol", None), P("pcol", None), P(("prow", "pcol"), None))
    return jax.shard_map(local, mesh=mesh, in_specs=in_specs, out_specs=out_specs, check_vma=False)
```

```python
import jax
import jax.numpy as jnp
from jax import lax
from jax.experimental import pallas as pl
from jax.experimental.pallas import tpu as pltpu
from jax.sharding import PartitionSpec as P

MESH = pl.DeviceIdType.MESH
F32 = jnp.float32
BF16 = jnp.bfloat16
NX = 8
FAR_FIRST = (4, 3, 5, 2, 6, 1, 7)
N_GROUPS = 44
PIECES = (pl.ds(0, 48), pl.ds(48, 40))


def kernel(
    r1_hbm, r2_hbm, rest_hbm, inv1_hbm, inv2_hbm, cross_hbm, pf_hbm, ps_hbm,
    o1_hbm, o2_hbm, o3_hbm,
    r1, r2, rest, inv1, inv2, cross, pf, ps,
    part, rs1, mid, rs2, full, rounded,
    cpart, yrs, sec,
    acc, pin, ring_in, ring_out, out,
    load_sem, store_sem, send_sem, recv_sem, pin_sem, ring_sem,
):
    r = lax.axis_index("prow")
    p = lax.axis_index("pcol")
    x, z = r // NX, r % NX
    y, c = p // 2, p % 2
    mine = (x, z)

    def at_x(k):
        return (lax.rem(x + k, NX) * NX + z, p)

    def at_z(k):
        return (x * NX + lax.rem(z + k, NX), p)

    def at_y(k, other_core=0):
        return (r, lax.rem(y + k, NX) * 2 + (1 - c if other_core else c))

    partner = at_y(0, 1)
    column = [(k, f) for k in FAR_FIRST for f in range(2)] + [(0, 1)]
    line = (at_x, at_z)

    def rows(start, count):
        return pl.ds(pl.multiple_of(start, 8), count)

    loads = []
    for i, (src, dst) in enumerate(
        ((inv1_hbm, inv1), (r1_hbm, r1), (cross_hbm, cross), (r2_hbm, r2),
         (inv2_hbm, inv2), (pf_hbm, pf), (ps_hbm, ps), (rest_hbm, rest))
    ):
        cp = pltpu.make_async_copy(src, dst, load_sem.at[i])
        cp.start()
        loads.append(cp)

    barrier = pltpu.get_barrier_semaphore()
    for k in range(1, NX):
        for to in line:
            pl.semaphore_signal(barrier, inc=1, device_id=to(k), device_id_type=MESH)
    for k, f in column:
        pl.semaphore_signal(barrier, inc=1, device_id=at_y(k, f), device_id_type=MESH)

    def send(src, dst, group, device, recv=None):
        pltpu.make_async_remote_copy(
            src_ref=src,
            dst_ref=dst,
            send_sem=send_sem.at[group],
            recv_sem=recv_sem.at[group] if recv is None else recv,
            device_id=device,
            device_id_type=MESH,
        ).start()

    def wait_bytes(ref, sem):
        pltpu.make_async_copy(ref, ref, sem).wait()

    at_end = []
    stores = []

    def arrived(ref, group):
        wait_bytes(ref, recv_sem.at[group])
        at_end.append(lambda: wait_bytes(ref, send_sem.at[group]))

    def solve(b, s):
        def group(stage, h):
            return ((b * 2 + s) * 4 + stage) * 2 + h

        if s == 1:
            for h in range(2):
                wait_bytes(rs1.at[b, 0, h], send_sem.at[(b * 16 + 0) + h])
        for k in FAR_FIRST:
            for h in range(2):
                to = lax.rem(mine[h] + k, NX)
                send(part.at[b, s, rows(h * 256 + to * 32, 32)], rs1.at[b, s, h, k - 1], group(0, h), line[h](k))
        yield
        for h in range(2):
            if s == 1:
                arrived(rs1.at[b, s, h], group(0, h))
            else:
                wait_bytes(rs1.at[b, s, h], recv_sem.at[group(0, h)])
            value = part[b, s, rows(h * 256 + mine[h] * 32, 32)]
            for k in range(1, NX):
                value = value + rs1[b, s, h, k - 1]
            other = mine[1 - h]
            mid[b, s, h] = value
            rs2[b, s, h, other] = value
            for k in FAR_FIRST:
                send(mid.at[b, s, h], rs2.at[b, s, h, other], group(1, h), line[1 - h](k))
        yield
        for h in range(2):
            arrived(rs2.at[b, s, h, pl.ds(0, 7)], group(1, h))
            value = rs2[b, s, h, 0]
            for i in range(1, NX):
                value = value + rs2[b, s, h, i]
            place = rows(h * 256 + mine[h] * 32, 32)
            full[b, s, place] = value
            here = full.at[b, s, place]
            for k in FAR_FIRST:
                send(here, here, group(3, h), line[h](k))
        yield
        for h in range(2):
            arrived(full.at[b, s, pl.ds(0, 224)], group(3, h))
        rounded[b, :, s * 128 : (s + 1) * 128] = full[b, s].astype(BF16)

    def store(b, s, out_hbm):
        cp = pltpu.make_async_copy(full.at[b, s], out_hbm.at[:, pl.ds(s * 128, 128)], store_sem.at[2 * b + s])
        cp.start()
        stores.append(cp)

    def first_update(i, carry):
        update = jnp.dot(pf[pl.ds(pl.multiple_of(i * 176, 176), 176)], rounded[0], preferred_element_type=F32)
        for core in range(2):
            for h in range(2):
                acc[i, core, h] = update[core * 88 : (core + 1) * 88, h * 128 : (h + 1) * 128]
        return carry

    def first_updates(low, high):
        for i in range(low, high):
            first_update(i, 0)

    up, down = at_y(1), at_y(NX - 1)

    def stream(s):
        columns = slice(s * 128, (s + 1) * 128)
        yield from solve(0, s)

        g = 32 + 4 * s
        if s == 0:
            loads[2].wait()
        cpart[s] = jnp.dot(cross[...], rounded[0, :, columns], preferred_element_type=F32)
        for k, f in column:
            to = at_y(k, f)
            send(cpart.at[s, rows(to[1] * 8, 8)], yrs.at[s, 2 * k + f - 1], g, to)
        store(0, s, o1_hbm)
        if s == 1:
            loads[5].wait()
            first_updates(0, 2)
        yield
        if s == 0:
            loads[3].wait()
        arrived(yrs.at[s], g)
        place = rows(p * 8, 8)
        value = cpart[s, place]
        for i in range(15):
            value = value + yrs[s, i]
        sec[s, place] = r2[place, columns] - value
        here = sec.at[s, place]
        for k, f in column:
            send(here, here, g + 1, at_y(k, f))
        if s == 1:
            first_updates(2, 4)
        yield
        if s == 0:
            loads[4].wait()
        arrived(sec.at[s, pl.ds(0, 120)], g + 1)
        part[1, s] = jnp.dot(inv2[...], sec[s].astype(BF16), preferred_element_type=F32)
        solving = solve(1, s)
        next(solving)
        if s == 1:
            first_updates(4, 8)
        yield
        yield from solving

        store(1, s, o2_hbm)
        if s == 0:
            loads[6].wait()

        def second_update(ks):
            for k in ks:
                to = lax.rem(y + k, NX)
                update = jnp.dot(ps[pl.ds(pl.multiple_of(to * 176, 176), 176)], rounded[1, :, columns], preferred_element_type=F32)
                for core in range(2):
                    acc[to, core, s] += update[core * 88 : (core + 1) * 88]
                send(acc.at[to, 1 - c, s], pin.at[k, s], 40 + s, partner, pin_sem.at[k, s])

        ready = set()

        def summed(k, part_rows):
            if k not in ready:
                wait_bytes(pin.at[k, s], pin_sem.at[k, s])
                ready.add(k)
            return acc[lax.rem(y + k, NX), c, s, part_rows] + pin[k, s, part_rows]

        slots = iter(range(7))

        def pass_on(step, way):
            slot = next(slots)
            for i, part_rows in enumerate(PIECES):
                value = summed(5 - step if way == 0 else NX - (5 - step), part_rows)
                if step > (1 if way == s else 2):
                    come = ring_in.at[way, step - 2, s, part_rows]
                    wait_bytes(come, ring_sem.at[way, step - 2, s, i])
                    value = value + come[...]
                ring_out[s, slot, part_rows] = value
                send(
                    ring_out.at[s, slot, part_rows], ring_in.at[way, step - 1, s, part_rows], 42 + s,
                    (up, down)[way], ring_sem.at[way, step - 1, s, i],
                )

        second_update((4, 3, 5, 2) if s == 0 else (4, 5, 3, 6))
        pass_on(1, s)
        pass_on(2, 1 - s)
        second_update((6, 1, 7, 0) if s == 0 else (2, 7, 1, 0))
        yield
        pass_on(2, s)
        yield
        pass_on(3, 1 - s)
        pass_on(3, s)
        yield
        pass_on(4, 1 - s)
        pass_on(4, s)
        yield
        if s == 0:
            loads[7].wait()
        for i, part_rows in enumerate(PIECES):
            value = summed(0, part_rows)
            for way in range(2):
                come = ring_in.at[way, 3, s, part_rows]
                wait_bytes(come, ring_sem.at[way, 3, s, i])
                value = value + come[...]
            out[s, part_rows] = rest[part_rows, columns] - value
        cp = pltpu.make_async_copy(out.at[s], o3_hbm.at[:, pl.ds(s * 128, 128)], store_sem.at[4 + s])
        cp.start()
        stores.append(cp)
        at_end.append(lambda: wait_bytes(pin.at[:, s], send_sem.at[40 + s]))
        at_end.append(lambda: wait_bytes(ring_out.at[s], send_sem.at[42 + s]))

    loads[0].wait()
    loads[1].wait()
    total = jnp.dot(inv1[...], r1[...].astype(BF16), preferred_element_type=F32)
    part[0, 0] = total[:, :128]
    part[0, 1] = total[:, 128:]
    pl.semaphore_wait(barrier, 2 * (NX - 1) + len(column))
    streams = [stream(0), stream(1)]
    while streams:
        for one in list(streams):
            try:
                next(one)
            except StopIteration:
                streams.remove(one)
    for end in at_end:
        end()
    for cp in stores:
        cp.wait()


def copy_kernel(a1, a2, a3, b1, b2, b3, v1, v2, v3, in_sem, out_sem):
    pieces = [(a3, v3, b3)]
    for i in range(4):
        rows = pl.ds(i * 128, 128)
        pieces += [(a1.at[rows], v1.at[rows], b1.at[rows]), (a2.at[rows], v2.at[rows], b2.at[rows])]
    come = [pltpu.make_async_copy(a, v, in_sem.at[i]) for i, (a, v, b) in enumerate(pieces)]
    go = [pltpu.make_async_copy(v, b, out_sem.at[i]) for i, (a, v, b) in enumerate(pieces)]
    for cp in come:
        cp.start()
    for cp, then in zip(come, go):
        cp.wait()
        then.start()
    for cp in go:
        cp.wait()


def solution(mesh):
    def local(rhs_first, rhs_second, rhs_rest, inverse_first, inverse_second, panel_cross, panel_first, panel_second):
        any_spec = pl.BlockSpec(memory_space=pltpu.HBM)
        arguments = (rhs_first, rhs_second, rhs_rest, inverse_first, inverse_second, panel_cross, panel_first, panel_second)
        shapes = (
            jax.ShapeDtypeStruct((512, 256), F32),
            jax.ShapeDtypeStruct((512, 256), F32),
            jax.ShapeDtypeStruct((88, 256), F32),
        )
        results = pl.pallas_call(
            kernel,
            out_shape=shapes,
            in_specs=[any_spec] * 8,
            out_specs=(any_spec,) * 3,
            scratch_shapes=[pltpu.VMEM(a.shape, a.dtype) for a in arguments]
            + [
                pltpu.VMEM((2, 2, 512, 128), F32),
                pltpu.VMEM((2, 2, 2, 7, 32, 128), F32),
                pltpu.VMEM((2, 2, 2, 32, 128), F32),
                pltpu.VMEM((2, 2, 2, 8, 32, 128), F32),
                pltpu.VMEM((2, 2, 512, 128), F32),
                pltpu.VMEM((2, 512, 256), BF16),
                pltpu.VMEM((2, 128, 128), F32),
                pltpu.VMEM((2, 15, 8, 128), F32),
                pltpu.VMEM((2, 128, 128), F32),
                pltpu.VMEM((8, 2, 2, 88, 128), F32),
                pltpu.VMEM((8, 2, 88, 128), F32),
                pltpu.VMEM((2, 4, 2, 88, 128), F32),
                pltpu.VMEM((2, 7, 88, 128), F32),
                pltpu.VMEM((2, 88, 128), F32),
                pltpu.SemaphoreType.DMA((8,)),
                pltpu.SemaphoreType.DMA((6,)),
                pltpu.SemaphoreType.DMA((N_GROUPS,)),
                pltpu.SemaphoreType.DMA((N_GROUPS,)),
                pltpu.SemaphoreType.DMA((8, 2)),
                pltpu.SemaphoreType.DMA((2, 4, 2, len(PIECES))),
            ],
            compiler_params=pltpu.CompilerParams(
                collective_id=0, has_side_effects=True, vmem_limit_bytes=60 * 2**20
            ),
            cost_estimate=pl.CostEstimate(flops=10**9, bytes_accessed=5 * 10**6, transcendentals=0),
        )(*arguments)
        return pl.pallas_call(
            copy_kernel,
            out_shape=shapes,
            in_specs=[any_spec] * 3,
            out_specs=(any_spec,) * 3,
            scratch_shapes=[pltpu.VMEM(a.shape, a.dtype) for a in shapes]
            + [pltpu.SemaphoreType.DMA((9,)), pltpu.SemaphoreType.DMA((9,))],
            compiler_params=pltpu.CompilerParams(vmem_limit_bytes=60 * 2**20),
        )(*results)

    in_specs = (
        P("prow", None),
        P("prow", None),
        P(("prow", "pcol"), None),
        P("pcol", "prow"),
        P("pcol", "prow"),
        P("prow", "pcol"),
        P("prow", "pcol"),
        P("prow", "pcol"),
    )
    out_specs = (P("pcol", None), P("pcol", None), P(("prow", "pcol"), None))
    return jax.shard_map(local, mesh=mesh, in_specs=in_specs, out_specs=out_specs, check_vma=False)
```
